32 devices in a mesh: groups: 2 (over x), row: 16 (over z, y, core), col: 1.
Axes of the slice: x: 2, y: 2, z: 4, core: 2. Of those that a mesh axis runs over, the one named last changes fastest.
Arguments:
- tokens: bfloat16 [512, 5120], P(('groups', 'row')), parts along dimension 0, may hold values from -6 to 6
- hidden_gradient: bfloat16 [512, 24576], P('groups', ('row', 'col')), parts along dimension 0, may hold values from -6 to 6
- gate_projection_weight: bfloat16 [24576, 5120], P(('row', 'col')), may hold values from -0.078125 to 0.078125
- up_projection_weight: bfloat16 [24576, 5120], P(('row', 'col')), may hold values from -0.078125 to 0.078125
- adapter_down_maps: bfloat16 [32, 5120, 16], P(('groups', 'row', 'col')), parts along dimension 0, may hold values from -0.078125 to 0.078125
- adapter_up_maps: bfloat16 [32, 16, 24576], P(('groups', 'row', 'col')), parts along dimension 0, may hold values from -1.5 to 1.5
- padded_block_tenant: int32 [4], P('groups'), parts along dimension 0, may hold values from 0 to 15
- tenant_adapter_slot: int32 [32], P('groups'), parts along dimension 0, may hold values from 0 to 15, each once
- block_live_count: int32 [4], P('groups'), parts along dimension 0, may hold values from 1 to 128, 192 in all
Outputs:
- input_gradient: bfloat16 [512, 5120], P(('groups', 'row', 'col')), parts along dimension 0
- down_grad: bfloat16 [32, 5120, 16], P(('groups', 'row', 'col')), parts along dimension 0
- up_grad: bfloat16 [32, 16, 24576], P(('groups', 'row', 'col')), parts along dimension 0
The draws below stay inside these ranges and needn't reach their ends.
There are 2 independent parts, one for each index of `groups`. The reference program is written for one: setup_inputs(seed, part) draws one part's arguments, and reference() takes and returns one part's arrays. A program takes and returns all parts, laid end to end along the dimension named above; an argument that names none is the same for every part. Nothing has to cross between parts.
All inputs are finite; a program needn't handle non-finite values.
Results may differ from the reference program's by a relative error of at most 0.006.
Values may be sent and summed in bfloat16 or wider, within the bound.
A program may use at most 192 MiB of HBM per device.

```python
import math
import jax
import jax.numpy as jnp
import numpy as np

FEATURE_WIDTH = 5120
HIDDEN_UNITS = 24576
ADAPTER_RANK = 16
BLOCK = 128
TOKEN_COUNT = 256
NBLK = 2
TENANT_COUNT = 16


def raised(drawn, own_key, source, target, shards_of, factor):
    def block_of(dim):
        return (jnp.arange(drawn.shape[dim]) // (drawn.shape[dim] // shards_of)).reshape((-1,) + (1,) * (drawn.ndim - 1 - dim))

    near = jax.random.permutation(own_key, shards_of)[block_of(target)]
    far = (block_of(target) + shards_of // 2) % shards_of
    return jnp.where((block_of(source) == near) | (block_of(source) == far), factor * drawn, drawn)


def block_scale(own_key, extent, cuts, least, top_value):
    def one(axis_at, blocks):
        steps = jax.random.uniform(jax.random.fold_in(jax.random.fold_in(own_key, 6), axis_at), (blocks,), jnp.float32, least / len(cuts), top_value / len(cuts))
        return jnp.repeat(jnp.exp(steps), extent[axis_at] // blocks).reshape((-1,) + (1,) * (len(extent) - axis_at - 1))

    loudness = one(*cuts[0])
    for cut in cuts[1:]:
        loudness = loudness * one(*cut)
    return loudness


def rank_bounds(count, lean):
    portions = [(1 << 20) // math.isqrt(rank ** lean) + 1 for rank in range(1, count + 1)]
    scale = 1 + sum(portions) // (1 << 30)
    return np.cumsum(np.array([max(1, weight // scale) for weight in portions]))


def ranked_ids(key, dims, count, lean):
    listing = rank_bounds(count, lean)
    pick = jax.random.randint(jax.random.fold_in(key, 1), dims, 0, int(listing[count - 1]))
    grade = jnp.searchsorted(jnp.asarray(listing, jnp.int32), pick, side="right")
    return jax.random.permutation(jax.random.fold_in(key, 2), count)[grade].astype(jnp.int32)


def profile(amount, total, most, skew):
    loads = [(1 << 20) // math.isqrt(standing ** skew) + 1 for standing in range(2, amount + 1)]
    rest, counts = total - most - (amount - 1), [1] * (amount - 1)
    while rest > 0:
        candidates = [i for i in range(amount - 1) if counts[i] < most]
        pool, budget = sum([loads[i] for i in candidates]), rest
        for i in candidates:
            extra = min(most - counts[i], max(1, budget * loads[i] // pool), rest)
            counts[i] = counts[i] + extra
            rest = rest - extra
    return np.array([most] + counts)


def ragged(stream_key, number_of, total, limit, skew):
    if number_of == 2:
        one = jax.random.randint(stream_key, (), max(1, total - limit), min(limit, total - 1) + 1)
        return jnp.stack([one, total - one])
    sizes = jnp.asarray(profile(number_of, total, limit, skew), jnp.int32)
    twos = (number_of - 1) // 2
    source_of, receiver = sizes[1:1 + 2 * twos:2], sizes[2:2 + 2 * twos:2]
    margin = jnp.minimum(source_of - 1, limit - receiver)
    shifted = jax.random.randint(jax.random.fold_in(stream_key, 1), (twos,), 0, 1 << 20) % (margin + 1)
    sizes = sizes.at[1:1 + 2 * twos:2].set(source_of - shifted).at[2:2 + 2 * twos:2].set(receiver + shifted)
    return sizes[jax.random.permutation(jax.random.fold_in(stream_key, 2), number_of)]


def gaussian(own_key, shape, scale, bound, split=(), kind=jnp.bfloat16):
    entries = jax.random.normal(own_key, shape, jnp.float32) * scale
    if len(split) > 0:
        entries = block_scale(own_key, shape, split, -0.22, 0.18) * entries
    return jnp.clip(entries, min=-bound, max=bound).astype(kind)


def heavy_noise(own_key, shape, deviation, bound, shards, heavy, kind=jnp.bfloat16):
    entries = deviation * jax.random.normal(own_key, shape, jnp.float32)
    if shards:
        entries = entries * block_scale(own_key, shape, shards, -0.22, 0.18)
    return jnp.clip(raised(entries, jax.random.fold_in(own_key, 3), *heavy), -bound, bound).astype(kind)


def setup_inputs(seed: int = 0, part: int = 0) -> dict:
    key_of = jax.random.split(jax.random.key(seed), 10)
    own_keys = jax.random.split(jax.random.fold_in(key_of[9], part), 10)
    tokens = gaussian(own_keys[0], (TOKEN_COUNT, FEATURE_WIDTH), 1.0, 6.0, ((0, 16),))
    hidden_gradient = heavy_noise(own_keys[1], (TOKEN_COUNT, HIDDEN_UNITS), 1.0, 6.0, ((1, 16),), (1, 0, 16, 2.0))
    gate_projection_weight = gaussian(key_of[2], (HIDDEN_UNITS, FEATURE_WIDTH), FEATURE_WIDTH ** -0.5, 0.078125, ((0, 16),))
    up_projection_weight = gaussian(key_of[3], (HIDDEN_UNITS, FEATURE_WIDTH), FEATURE_WIDTH ** -0.5, 0.078125, ((0, 16),))
    adapter_down_maps = gaussian(own_keys[4], (TENANT_COUNT, FEATURE_WIDTH, ADAPTER_RANK), FEATURE_WIDTH ** -0.5, 0.078125, ((0, 16),))
    adapter_up_maps = gaussian(own_keys[5], (TENANT_COUNT, ADAPTER_RANK, HIDDEN_UNITS), ADAPTER_RANK ** -0.5, 1.5, ((0, 16),))
    padded_block_tenant = ranked_ids(own_keys[6], (NBLK,), TENANT_COUNT, 2)
    tenant_adapter_slot = jax.random.permutation(own_keys[7], TENANT_COUNT).astype(jnp.int32)
    block_live_count = ragged(own_keys[8], NBLK, (BLOCK // 2) * NBLK + BLOCK // 2, BLOCK, 1).astype(jnp.int32)
    return {"tokens": tokens, "hidden_gradient": hidden_gradient, "gate_projection_weight": gate_projection_weight, "up_projection_weight": up_projection_weight, "adapter_down_maps": adapter_down_maps, "adapter_up_maps": adapter_up_maps, "padded_block_tenant": padded_block_tenant, "tenant_adapter_slot": tenant_adapter_slot, "block_live_count": block_live_count}


ADAPTER_SCALE = 0.5


def reference(tokens, hidden_gradient, gate_projection_weight, up_projection_weight, adapter_down_maps, adapter_up_maps, padded_block_tenant, tenant_adapter_slot, block_live_count):
    num_blocks = TOKEN_COUNT // BLOCK
    block_adapter_slot = tenant_adapter_slot[padded_block_tenant]
    adapter_down_blocks = adapter_down_maps[block_adapter_slot].astype(jnp.float32)
    adapter_up_blocks = adapter_up_maps[block_adapter_slot].astype(jnp.float32)
    token_block_groups = tokens.astype(jnp.float32).reshape(num_blocks, BLOCK, FEATURE_WIDTH)
    latent_rows = jnp.einsum("bid,bdr->bir", token_block_groups, adapter_down_blocks).astype(jnp.bfloat16)
    adapter_gate_term = jnp.einsum("lme,leq->lmq", latent_rows.astype(jnp.float32), adapter_up_blocks).reshape(TOKEN_COUNT, HIDDEN_UNITS)
    gate_activation = jnp.dot(tokens, gate_projection_weight.T, preferred_element_type=jnp.float32) + ADAPTER_SCALE * adapter_gate_term
    up_act = jnp.dot(tokens, up_projection_weight.T, preferred_element_type=jnp.float32)
    live_rows = (jnp.arange(BLOCK, dtype=jnp.int32)[None, :] < block_live_count[:, None]).reshape(TOKEN_COUNT).astype(jnp.float32)
    sigmoid_gate = jax.nn.sigmoid(gate_activation)
    masked_grad = hidden_gradient.astype(jnp.float32) * live_rows[:, None]
    dgate = (masked_grad * up_act * sigmoid_gate * (1.0 + gate_activation * (1.0 - sigmoid_gate))).astype(jnp.bfloat16)
    dup = (masked_grad * gate_activation * sigmoid_gate).astype(jnp.bfloat16)
    primary_term = jnp.dot(dgate, gate_projection_weight, preferred_element_type=jnp.float32) + jnp.dot(dup, up_projection_weight, preferred_element_type=jnp.float32)
    gate_gradient_blocks = dgate.astype(jnp.float32).reshape(num_blocks, BLOCK, HIDDEN_UNITS)
    latent_gradient = jnp.einsum("bif,brf->bir", gate_gradient_blocks, adapter_up_blocks).astype(jnp.bfloat16)
    adapter_input_term = jnp.einsum("tqy,tly->tql", latent_gradient.astype(jnp.float32), adapter_down_blocks).reshape(TOKEN_COUNT, FEATURE_WIDTH)
    input_gradient = (primary_term + ADAPTER_SCALE * adapter_input_term).astype(jnp.bfloat16)
    blockwise_down_maps = ADAPTER_SCALE * jnp.einsum("qes,qen->qsn", token_block_groups, latent_gradient.astype(jnp.float32))
    blockwise_up_maps = ADAPTER_SCALE * jnp.einsum("zde,zdk->zek", latent_rows.astype(jnp.float32), gate_gradient_blocks)
    down_grad = jax.ops.segment_sum(blockwise_down_maps, block_adapter_slot, TENANT_COUNT).astype(jnp.bfloat16)
    up_grad = jax.ops.segment_sum(blockwise_up_maps, block_adapter_slot, TENANT_COUNT).astype(jnp.bfloat16)
    return input_gradient, down_grad, up_grad
```

```python
import functools

import jax
import jax.numpy as jnp
from jax import lax
from jax.experimental import pallas as pl
from jax.experimental.pallas import tpu as pltpu
from jax.sharding import PartitionSpec as P

BLOCK = 128
ADAPTER_SCALE = 0.5
CHUNKS = 4
BF16 = jnp.bfloat16
F32 = jnp.float32


def dot(a, b, ca, cb):
    return lax.dot_general(a, b, (((ca,), (cb,)), ((), ())), preferred_element_type=F32)


def each(lo, hi, body):
    def step(i, carry):
        body(i)
        return carry

    lax.fori_loop(lo, hi, step, 0)


def kernel(
    dims,
    tok_in, hid_ref, gate_hbm, up_hbm, down_ref, maps_ref, tenant_ref, slot_ref, live_ref,
    din_ref, ddown_ref, dmaps_ref,
    wg, wu, tok, acc_g, acc_u, dgate, dup, part,
    cs_buf, cr_buf, ys_buf, yr_buf, zs_buf, zr_buf,
    mcs_buf, mcr_buf, mys_buf, myr_buf, mzs_buf, mzr_buf, maps,
    codes_buf, cgrad_buf, ugrad_buf,
    w_sem, tz_sem, ty_sem, tc_sem, uz_sem, uy_sem, uc_sem,
    rc_sem, ry_sem, rz_sem, mc_sem, my_sem, mz_sem, code_sem, cgrad_sem,
):
    nz, ny, ncol = dims
    n = nz * ny * 2
    rows, width = tok_in.shape
    total = n * rows
    blocks = total // BLOCK
    hidden = wg.shape[0]
    rank = down_ref.shape[0]
    cw = width // CHUNKS
    me = lax.axis_index("row") * ncol + lax.axis_index("col")
    z, y, c = me // (2 * ny), (me // 2) % ny, me % 2

    def index(zz, yy, cc):
        return (zz * ny + yy) * 2 + cc

    def device(i):
        return {"row": i // ncol, "col": i % ncol}

    def remote(src, dst, sems, target):
        return pltpu.make_async_remote_copy(
            src_ref=src,
            dst_ref=dst,
            send_sem=sems[0],
            recv_sem=sems[1],
            device_id=device(target),
            device_id_type=pl.DeviceIdType.MESH,
        )

    y_peer, c_peer = index(z, ny - 1 - y, c), index(z, y, 1 - c)

    def weight_copy(k, which):
        src, dst = ((gate_hbm, wg), (up_hbm, wu))[which]
        cols = pl.ds(k * cw, cw)
        return pltpu.make_async_copy(src.at[:, cols], dst.at[:, cols], w_sem.at[k, which])

    for k in range(CHUNKS):
        for which in range(2):
            weight_copy(k, which).start()

    barrier = pltpu.get_barrier_semaphore()

    def greet(d):
        pl.semaphore_signal(
            barrier, inc=1, device_id=device((me + d) % n), device_id_type=pl.DeviceIdType.MESH
        )

    each(1, n, greet)
    tok[me] = tok_in[...]
    pl.semaphore_wait(barrier, n - 1)

    class Gather:
        def __init__(self, view, zsem, ysem, csem, k):
            self.view, self.k = view, k
            self.zsem, self.ysem, self.csem = zsem, ysem, csem

        def z_copy(self, d, shard):
            sems = (self.zsem.at[0, self.k, d], self.zsem.at[1, self.k, d])
            v = self.view(shard)
            return remote(v, v, sems, index((z + d) % nz, y, c))

        def y_copy(self, d, shard):
            sems = (self.ysem.at[0, self.k, d], self.ysem.at[1, self.k, d])
            v = self.view(shard)
            return remote(v, v, sems, y_peer)

        def c_copy(self, j, shard):
            sems = (self.csem.at[0, self.k, j], self.csem.at[1, self.k, j])
            v = self.view(shard)
            return remote(v, v, sems, c_peer)

        def start(self):
            each(1, nz, lambda d: self.z_copy(d, me).start())
            if ny > 1:
                self.y_copy(0, me).start()
            self.c_copy(0, me).start()

        def on_z(self):
            def arrived(d):
                shard = index((z + nz - d) % nz, y, c)
                self.z_copy(d, shard).wait_recv()
                if ny > 1:
                    self.y_copy(d, shard).start()
                self.c_copy(d, shard).start()

            each(1, nz, arrived)

        def on_y(self):
            def arrived(d):
                shard = index((z + nz - d) % nz, ny - 1 - y, c)
                self.y_copy(d, shard).wait_recv()
                self.c_copy(nz + d, shard).start()

            if ny > 1:
                each(0, nz, arrived)

        def on_c(self):
            each(0, nz * ny, lambda j: self.c_copy(j, me).wait_recv())

        def finish(self):
            each(1, nz, lambda d: self.z_copy(d, me).wait_send())
            if ny > 1:
                each(0, nz, lambda d: self.y_copy(d, me).wait_send())
            each(0, nz * ny, lambda j: self.c_copy(j, me).wait_send())

    class Reduce:
        def __init__(self, piece, bufs, sems, k):
            self.piece, self.k = piece, k
            self.cs, self.cr, self.ys, self.yr, self.zs, self.zr = [b.at[k] for b in bufs]
            csem, ysem, zsem = sems
            self.c_copy = remote(self.cs, self.cr, (csem.at[0, k], csem.at[1, k]), c_peer)
            self.y_copy = remote(self.ys, self.yr, (ysem.at[0, k], ysem.at[1, k]), y_peer)
            self.zsem = zsem

        def z_copy(self, d):
            sems = (self.zsem.at[0, self.k, d], self.zsem.at[1, self.k, d])
            return remote(self.zs.at[d], self.zr.at[d], sems, index((z + d) % nz, y, c))

        def start(self):
            def fill(j):
                self.cs[j] = self.piece(j * 2 + 1 - c).astype(BF16)

            each(0, nz * ny, fill)
            self.c_copy.start()

        def chip_sum(self, zz, yy):
            return self.piece(index(zz, yy, c)) + self.cr[zz * ny + yy].astype(F32)

        def on_c(self):
            self.c_copy.wait_recv()

            def fill(zz):
                self.ys[zz] = self.chip_sum(zz, ny - 1 - y).astype(BF16)

            if ny > 1:
                each(0, nz, fill)
                self.y_copy.start()

        def y_sum(self, zz):
            value = self.chip_sum(zz, y)
            if ny > 1:
                value = value + self.yr[zz].astype(F32)
            return value

        def on_y(self):
            if ny > 1:
                self.y_copy.wait_recv()

            def send(d):
                self.zs[d] = self.y_sum((z + d) % nz).astype(BF16)
                self.z_copy(d).start()

            each(1, nz, send)

        def result(self):
            def add(d, value):
                self.z_copy(d).wait_recv()
                return value + self.zr[d].astype(F32)

            return lax.fori_loop(1, nz, add, self.y_sum(z))

        def finish(self):
            self.c_copy.wait_send()
            if ny > 1:
                self.y_copy.wait_send()
            each(1, nz, lambda d: self.z_copy(d).wait_send())

    def to_all(buf, sem):
        def copy(d, shard):
            return remote(buf.at[shard], buf.at[shard], (sem.at[0, d], sem.at[1, d]), (me + d) % n)

        return (
            lambda: each(1, n, lambda d: copy(d, me).start()),
            lambda: each(1, n, lambda d: copy(d, (me + n - d) % n).wait_recv()),
            lambda: each(1, n, lambda d: copy(d, me).wait_send()),
        )

    slots = [slot_ref[tenant_ref[b]] for b in range(blocks)]
    chosen = [jnp.where(s == me, 1.0, 0.0).astype(F32) for s in slots]
    token_block = lax.broadcasted_iota(jnp.int32, (1, total), 1) // BLOCK
    token_chosen = jnp.zeros((1, total), F32)
    for b in range(blocks):
        token_chosen = jnp.where(token_block == b, chosen[b], token_chosen)

    def map_piece(i):
        cols = pl.ds(pl.multiple_of(i * hidden, 128), hidden)
        one = maps_ref[:, cols].astype(F32)
        return jnp.concatenate([one * chosen[b] for b in range(blocks)], axis=0)

    map_reduce = Reduce(
        map_piece,
        (mcs_buf, mcr_buf, mys_buf, myr_buf, mzs_buf, mzr_buf),
        (mc_sem, my_sem, mz_sem),
        0,
    )
    gathers = [
        Gather(
            lambda shard, k=k: tok.at[shard, :, pl.ds(k * cw, cw)], tz_sem, ty_sem, tc_sem, k
        )
        for k in range(CHUNKS)
    ]

    for g in gathers:
        g.start()
    map_reduce.start()

    tile = min(hidden, 512)
    half = min(hidden, 256) if hidden % 256 == 0 else 128

    def token_chunk(k):
        return tok[:, :, k * cw:(k + 1) * cw].reshape(total, cw)

    def forward(k):
        weight_copy(k, 0).wait()
        weight_copy(k, 1).wait()
        tk = token_chunk(k)

        def step(t):
            span = pl.ds(pl.multiple_of(t * tile, 128), tile)
            g = dot(tk, wg[span, k * cw:(k + 1) * cw], 1, 1)
            u = dot(tk, wu[span, k * cw:(k + 1) * cw], 1, 1)
            if k == 0:
                acc_g[:, span] = g
                acc_u[:, span] = u
            else:
                acc_g[:, span] += g
                acc_u[:, span] += u

        each(0, hidden // tile, step)

    own_codes = jnp.zeros((rank, total), F32)
    for i in range(CHUNKS + 2):
        if i < CHUNKS:
            gathers[i].on_z()
        if i == CHUNKS - 1:
            map_reduce.on_c()
        if 0 <= i - 1 < CHUNKS:
            gathers[i - 1].on_y()
        if i == CHUNKS:
            map_reduce.on_y()
        if i >= 2:
            k = i - 2
            gathers[k].on_c()
            own_codes = own_codes + dot(
                down_ref[:, k * cw:(k + 1) * cw], token_chunk(k), 1, 1
            )
            if k == CHUNKS - 1:
                codes_start, codes_wait, codes_finish = to_all(codes_buf, code_sem)
                codes_buf[me] = (own_codes * token_chosen).astype(BF16)
                codes_start()
            forward(k)

    maps[...] = map_reduce.result().astype(BF16)
    codes_wait()
    codes = jnp.sum(codes_buf[...].astype(F32), axis=0).astype(BF16)

    for b in range(blocks):
        tokens_b = slice(b * BLOCK, (b + 1) * BLOCK)
        codes_b = codes[:, tokens_b]
        live = lax.broadcasted_iota(jnp.int32, (BLOCK, 1), 0) < live_ref[b]

        def activate(t, b=b, tokens_b=tokens_b, codes_b=codes_b, live=live):
            span = pl.ds(pl.multiple_of(t * half, 128), half)
            map_b = maps[b * rank:(b + 1) * rank, span]
            gate = acc_g[tokens_b, span] + ADAPTER_SCALE * dot(codes_b, map_b, 0, 0)
            s = 1.0 / (1.0 + jnp.exp(-gate))
            grad = jnp.where(live, hid_ref[tokens_b, span].astype(F32), 0.0)
            grad_s = grad * s
            dgate[tokens_b, span] = (
                grad_s * acc_u[tokens_b, span] * (1.0 + gate * (1.0 - s))
            ).astype(BF16)
            dup[tokens_b, span] = (grad_s * gate).astype(BF16)

        each(0, hidden // half, activate)

    cgrad_start, cgrad_wait, cgrad_finish = to_all(cgrad_buf, cgrad_sem)
    for b in range(blocks):
        tokens_b = slice(b * BLOCK, (b + 1) * BLOCK)
        cgrad_buf[me, :, tokens_b] = dot(
            maps[b * rank:(b + 1) * rank, :], dgate[tokens_b, :], 1, 1
        )
    cgrad_start()
    for b in range(blocks):
        tokens_b = slice(b * BLOCK, (b + 1) * BLOCK)
        ugrad_buf[me, b * rank:(b + 1) * rank, :] = (
            ADAPTER_SCALE * dot(codes[:, tokens_b], dgate[tokens_b, :], 1, 0)
        ).astype(BF16)
    ugather = Gather(lambda shard: ugrad_buf.at[shard], uz_sem, uy_sem, uc_sem, 0)
    ugather.start()

    ct = 256 if cw % 256 == 0 else 128

    def backward(k):
        def step(t):
            cols = pl.ds(pl.multiple_of(k * cw + t * ct, 128), ct)
            value = dot(dgate[...], wg[:, cols], 1, 0) + dot(dup[...], wu[:, cols], 1, 0)
            part[k, :, :, pl.ds(pl.multiple_of(t * ct, 128), ct)] = value.reshape(n, rows, ct)

        each(0, cw // ct, step)

    def add_adapter(k, cg):
        def step(t):
            cols = pl.ds(pl.multiple_of(k * cw + t * ct, 128), ct)
            span = pl.ds(pl.multiple_of(t * ct, 128), ct)
            value = ADAPTER_SCALE * dot(cg, down_ref[:, cols], 0, 0)
            part[k, :, :, span] += value.reshape(n, rows, ct)

        each(0, cw // ct, step)

    reduces = [
        Reduce(
            lambda i, k=k: part[k, i],
            (cs_buf, cr_buf, ys_buf, yr_buf, zs_buf, zr_buf),
            (rc_sem, ry_sem, rz_sem),
            k,
        )
        for k in range(CHUNKS)
    ]

    def store(k):
        din_ref[:, k * cw:(k + 1) * cw] = reduces[k].result().astype(BF16)

    cg = None
    for i in range(CHUNKS):
        backward(i)
        if i == 0:
            cgrad_wait()
            cg = jnp.sum(cgrad_buf[...], axis=0).astype(BF16).astype(F32)
            cg = (cg * token_chosen).astype(BF16)
            ugather.on_z()
        if i == 1:
            ugather.on_y()
        add_adapter(i, cg)
        reduces[i].start()
        if i >= 1:
            reduces[i - 1].on_c()
        if i >= 2:
            reduces[i - 2].on_y()
        if i >= 3:
            store(i - 3)
    last = CHUNKS - 1
    reduces[last].on_c()
    if last >= 1:
        reduces[last - 1].on_y()

    for k in range(CHUNKS):
        ddown_ref[:, k * cw:(k + 1) * cw] = (
            ADAPTER_SCALE * dot(cg, token_chunk(k), 1, 0)
        ).astype(BF16)
    reduces[last].on_y()

    ugather.on_c()

    def put(d):
        value = jnp.zeros((rank, hidden), F32)
        for b in range(blocks):
            value = value + chosen[b] * ugrad_buf[d, b * rank:(b + 1) * rank, :].astype(F32)
        dmaps_ref[:, pl.ds(pl.multiple_of(d * hidden, 128), hidden)] = value.astype(BF16)

    each(0, n, put)
    for k in range(max(0, CHUNKS - 3), CHUNKS):
        store(k)
    for g in gathers:
        g.finish()
    ugather.finish()
    map_reduce.finish()
    codes_finish()
    cgrad_finish()
    for r in reduces:
        r.finish()


def body(
    nrow,
    ncol,
    tokens,
    hidden_gradient,
    gate_projection_weight,
    up_projection_weight,
    adapter_down_maps,
    adapter_up_maps,
    padded_block_tenant,
    tenant_adapter_slot,
    block_live_count,
):
    n = nrow * ncol
    ny = 2 if ncol == 1 else 1
    nz = n // (2 * ny)
    rows = tokens.shape[0] // ncol
    if ncol > 1:
        tokens = lax.dynamic_slice_in_dim(tokens, lax.axis_index("col") * rows, rows, 0)
    width = tokens.shape[1]
    total = n * rows
    hidden = gate_projection_weight.shape[0]
    rank = adapter_up_maps.shape[1]
    blocks = total // BLOCK
    cw = width // CHUNKS
    mr = blocks * rank
    half = nz * ny
    vmem = pl.BlockSpec(memory_space=pltpu.VMEM)
    smem = pl.BlockSpec(memory_space=pltpu.SMEM)
    hbm = pl.BlockSpec(memory_space=pl.ANY)
    sem = pltpu.SemaphoreType.DMA
    scratch = [
        pltpu.VMEM((hidden, width), BF16),
        pltpu.VMEM((hidden, width), BF16),
        pltpu.VMEM((n, rows, width), BF16),
        pltpu.VMEM((total, hidden), F32),
        pltpu.VMEM((total, hidden), F32),
        pltpu.VMEM((total, hidden), BF16),
        pltpu.VMEM((total, hidden), BF16),
        pltpu.VMEM((CHUNKS, n, rows, cw), F32),
        pltpu.VMEM((CHUNKS, half, rows, cw), BF16),
        pltpu.VMEM((CHUNKS, half, rows, cw), BF16),
        pltpu.VMEM((CHUNKS, nz, rows, cw), BF16),
        pltpu.VMEM((CHUNKS, nz, rows, cw), BF16),
        pltpu.VMEM((CHUNKS, nz, rows, cw), BF16),
        pltpu.VMEM((CHUNKS, nz, rows, cw), BF16),
        pltpu.VMEM((1, half, mr, hidden), BF16),
        pltpu.VMEM((1, half, mr, hidden), BF16),
        pltpu.VMEM((1, nz, mr, hidden), BF16),
        pltpu.VMEM((1, nz, mr, hidden), BF16),
        pltpu.VMEM((1, nz, mr, hidden), BF16),
        pltpu.VMEM((1, nz, mr, hidden), BF16),
        pltpu.VMEM((mr, hidden), BF16),
        pltpu.VMEM((n, rank, total), BF16),
        pltpu.VMEM((n, rank, total), F32),
        pltpu.VMEM((n, mr, hidden), BF16),
        sem((CHUNKS, 2)),
        sem((2, CHUNKS, nz)),
        sem((2, CHUNKS, nz)),
        sem((2, CHUNKS, half)),
        sem((2, 1, nz)),
        sem((2, 1, nz)),
        sem((2, 1, half)),
        sem((2, CHUNKS)),
        sem((2, CHUNKS)),
        sem((2, CHUNKS, nz)),
        sem((2, 1)),
        sem((2, 1)),
        sem((2, 1, nz)),
        sem((2, n)),
        sem((2, n)),
    ]
    input_gradient, down_t, up_grad = pl.pallas_call(
        functools.partial(kernel, (nz, ny, ncol)),
        out_shape=(
            jax.ShapeDtypeStruct((rows, width), BF16),
            jax.ShapeDtypeStruct((rank, width), BF16),
            jax.ShapeDtypeStruct((rank, n * hidden), BF16),
        ),
        in_specs=[vmem, vmem, hbm, hbm, vmem, vmem, smem, smem, smem],
        out_specs=(vmem, vmem, vmem),
        scratch_shapes=scratch,
        compiler_params=pltpu.CompilerParams(
            collective_id=0, has_side_effects=True, vmem_limit_bytes=62 * 1024 * 1024
        ),
    )(
        tokens,
        hidden_gradient,
        gate_projection_weight,
        up_projection_weight,
        jnp.swapaxes(adapter_down_maps[0], 0, 1),
        adapter_up_maps[0],
        padded_block_tenant,
        tenant_adapter_slot,
        block_live_count,
    )
    return input_gradient, jnp.swapaxes(down_t, 0, 1)[None], up_grad[None]


def solution(mesh):
    return jax.shard_map(
        functools.partial(body, mesh.shape["row"], mesh.shape["col"]),
        mesh=mesh,
        in_specs=(
            P(("groups", "row"), None),
            P("groups", ("row", "col")),
            P(("row", "col"), None),
            P(("row", "col"), None),
            P(("groups", "row", "col"), None, None),
            P(("groups", "row", "col"), None, None),
            P("groups"),
            P("groups"),
            P("groups"),
        ),
        out_specs=(
            P(("groups", "row", "col"), None),
            P(("groups", "row", "col"), None, None),
            P(("groups", "row", "col"), None, None),
        ),
        check_vma=False,
    )
```

```python
import functools

import jax
import jax.numpy as jnp
from jax import lax
from jax.experimental import pallas as pl
from jax.experimental.pallas import tpu as pltpu
from jax.sharding import PartitionSpec as P

BLOCK = 128
ADAPTER_SCALE = 0.5
CHUNKS = 4
BF16 = jnp.bfloat16
F32 = jnp.float32


def dot(a, b, ca, cb):
    return lax.dot_general(a, b, (((ca,), (cb,)), ((), ())), preferred_element_type=F32)


def each(lo, hi, body):
    def step(i, carry):
        body(i)
        return carry

    lax.fori_loop(lo, hi, step, 0)


def kernel(
    dims,
    tok_in, hid_ref, gate_hbm, up_hbm, down_ref, maps_ref, tenant_ref, slot_ref, live_ref,
    din_ref, ddown_ref, dmaps_ref,
    wg, wu, tok, acc_g, acc_u, dgate, dup, part,
    cs_buf, cr_buf, ys_buf, yr_buf, zs_buf, zr_buf,
    mcs_buf, mcr_buf, mys_buf, myr_buf, mzs_buf, mzr_buf, maps,
    codes_buf, cgrad_buf, ugrad_buf,
    w_sem, tz_sem, ty_sem, tc_sem, uz_sem, uy_sem, uc_sem,
    rc_sem, ry_sem, rz_sem, mc_sem, my_sem, mz_sem, code_sem, cgrad_sem,
):
    nz, ny, ncol = dims
    n = nz * ny * 2
    rows, width = tok_in.shape
    total = n * rows
    blocks = total // BLOCK
    hidden = wg.shape[0]
    rank = down_ref.shape[0]
    cw = width // CHUNKS
    me = lax.axis_index("row") * ncol + lax.axis_index("col")
    z, y, c = me // (2 * ny), (me // 2) % ny, me % 2

    def index(zz, yy, cc):
        return (zz * ny + yy) * 2 + cc

    def device(i):
        return {"row": i // ncol, "col": i % ncol}

    def remote(src, dst, sems, target):
        return pltpu.make_async_remote_copy(
            src_ref=src,
            dst_ref=dst,
            send_sem=sems[0],
            recv_sem=sems[1],
            device_id=device(target),
            device_id_type=pl.DeviceIdType.MESH,
        )

    y_peer, c_peer = index(z, ny - 1 - y, c), index(z, y, 1 - c)

    def weight_copy(k, which):
        src, dst = ((gate_hbm, wg), (up_hbm, wu))[which]
        cols = pl.ds(k * cw, cw)
        return pltpu.make_async_copy(src.at[:, cols], dst.at[:, cols], w_sem.at[k, which])

    for k in range(CHUNKS):
        for which in range(2):
            weight_copy(k, which).start()

    barrier = pltpu.get_barrier_semaphore()

    def greet(d):
        pl.semaphore_signal(
            barrier, inc=1, device_id=device((me + d) % n), device_id_type=pl.DeviceIdType.MESH
        )

    each(1, n, greet)
    tok[me] = tok_in[...]
    pl.semaphore_wait(barrier, n - 1)

    class Gather:
        def __init__(self, view, zsem, ysem, csem, k):
            self.view, self.k = view, k
            self.zsem, self.ysem, self.csem = zsem, ysem, csem

        def z_copy(self, d, shard):
            sems = (self.zsem.at[0, self.k, d], self.zsem.at[1, self.k, d])
            v = self.view(shard)
            return remote(v, v, sems, index((z + d) % nz, y, c))

        def y_copy(self, d, shard):
            sems = (self.ysem.at[0, self.k, d], self.ysem.at[1, self.k, d])
            v = self.view(shard)
            return remote(v, v, sems, y_peer)

        def c_copy(self, j, shard):
            sems = (self.csem.at[0, self.k, j], self.csem.at[1, self.k, j])
            v = self.view(shard)
            return remote(v, v, sems, c_peer)

        def start(self):
            each(1, nz, lambda d: self.z_copy(d, me).start())
            if ny > 1:
                self.y_copy(0, me).start()
            self.c_copy(0, me).start()

        def on_z(self):
            def arrived(d):
                shard = index((z + nz - d) % nz, y, c)
                self.z_copy(d, shard).wait_recv()
                if ny > 1:
                    self.y_copy(d, shard).start()
                self.c_copy(d, shard).start()

            each(1, nz, arrived)

        def on_y(self):
            def arrived(d):
                shard = index((z + nz - d) % nz, ny - 1 - y, c)
                self.y_copy(d, shard).wait_recv()
                self.c_copy(nz + d, shard).start()

            if ny > 1:
                each(0, nz, arrived)

        def on_c(self):
            each(0, nz * ny, lambda j: self.c_copy(j, me).wait_recv())

        def finish(self):
            each(1, nz, lambda d: self.z_copy(d, me).wait_send())
            if ny > 1:
                each(0, nz, lambda d: self.y_copy(d, me).wait_send())
            each(0, nz * ny, lambda j: self.c_copy(j, me).wait_send())

    class Reduce:
        def __init__(self, piece, bufs, sems, k):
            self.piece, self.k = piece, k
            self.cs, self.cr, self.ys, self.yr, self.zs, self.zr = [b.at[k] for b in bufs]
            csem, ysem, zsem = sems
            self.c_copy = remote(self.cs, self.cr, (csem.at[0, k], csem.at[1, k]), c_peer)
            self.y_copy = remote(self.ys, self.yr, (ysem.at[0, k], ysem.at[1, k]), y_peer)
            self.zsem = zsem

        def z_copy(self, d):
            sems = (self.zsem.at[0, self.k, d], self.zsem.at[1, self.k, d])
            return remote(self.zs.at[d], self.zr.at[d], sems, index((z + d) % nz, y, c))

        def start(self):
            def fill(j):
                self.cs[j] = self.piece(j * 2 + 1 - c).astype(BF16)

            each(0, nz * ny, fill)
            self.c_copy.start()

        def chip_sum(self, zz, yy):
            return self.piece(index(zz, yy, c)) + self.cr[zz * ny + yy].astype(F32)

        def on_c(self):
            self.c_copy.wait_recv()

            def fill(zz):
                self.ys[zz] = self.chip_sum(zz, ny - 1 - y).astype(BF16)

            if ny > 1:
                each(0, nz, fill)
                self.y_copy.start()

        def y_sum(self, zz):
            value = self.chip_sum(zz, y)
            if ny > 1:
                value = value + self.yr[zz].astype(F32)
            return value

        def on_y(self):
            if ny > 1:
                self.y_copy.wait_recv()

            def send(d):
                self.zs[d] = self.y_sum((z + d) % nz).astype(BF16)
                self.z_copy(d).start()

            each(1, nz, send)

        def result(self):
            def add(d, value):
                self.z_copy(d).wait_recv()
                return value + self.zr[d].astype(F32)

            return lax.fori_loop(1, nz, add, self.y_sum(z))

        def finish(self):
            self.c_copy.wait_send()
            if ny > 1:
                self.y_copy.wait_send()
            each(1, nz, lambda d: self.z_copy(d).wait_send())

    class Sum:
        def __init__(self, buf, sem):
            self.buf, self.sem = buf, sem

        def pair(self, i, target):
            sems = (self.sem.at[0, i], self.sem.at[1, i])
            return remote(self.buf.at[2 * i], self.buf.at[2 * i + 1], sems, target)

        def z_copy(self, d):
            sems = (self.sem.at[0, 1 + d], self.sem.at[1, 1 + d])
            return remote(self.buf.at[4], self.buf.at[4 + d], sems, index((z + d) % nz, y, c))

        def start(self):
            self.pair(0, c_peer).start()

        def on_c(self):
            self.pair(0, c_peer).wait_recv()
            value = self.buf[0].astype(F32) + self.buf[1].astype(F32)
            self.buf[2] = value.astype(self.buf.dtype)
            if ny > 1:
                self.pair(1, y_peer).start()

        def on_y(self):
            value = self.buf[2].astype(F32)
            if ny > 1:
                self.pair(1, y_peer).wait_recv()
                value = value + self.buf[3].astype(F32)
            self.buf[4] = value.astype(self.buf.dtype)
            each(1, nz, lambda d: self.z_copy(d).start())

        def result(self):
            each(1, nz, lambda d: self.z_copy(d).wait_recv())
            return jnp.sum(self.buf[4:4 + nz].astype(F32), axis=0).astype(BF16)

        def finish(self):
            self.pair(0, c_peer).wait_send()
            if ny > 1:
                self.pair(1, y_peer).wait_send()
            each(1, nz, lambda d: self.z_copy(d).wait_send())

    slots = [slot_ref[tenant_ref[b]] for b in range(blocks)]
    chosen = [jnp.where(s == me, 1.0, 0.0).astype(F32) for s in slots]
    token_block = lax.broadcasted_iota(jnp.int32, (1, total), 1) // BLOCK
    token_chosen = jnp.zeros((1, total), F32)
    for b in range(blocks):
        token_chosen = jnp.where(token_block == b, chosen[b], token_chosen)

    def map_piece(i):
        cols = pl.ds(pl.multiple_of(i * hidden, 128), hidden)
        one = maps_ref[:, cols].astype(F32)
        return jnp.concatenate([one * chosen[b] for b in range(blocks)], axis=0)

    map_reduce = Reduce(
        map_piece,
        (mcs_buf, mcr_buf, mys_buf, myr_buf, mzs_buf, mzr_buf),
        (mc_sem, my_sem, mz_sem),
        0,
    )
    gathers = [
        Gather(
            lambda shard, k=k: tok.at[shard, :, pl.ds(k * cw, cw)], tz_sem, ty_sem, tc_sem, k
        )
        for k in range(CHUNKS)
    ]

    for g in gathers:
        g.start()
    map_reduce.start()

    tile = min(hidden, 512)
    half = min(hidden, 256) if hidden % 256 == 0 else 128

    def token_chunk(k):
        return tok[:, :, k * cw:(k + 1) * cw].reshape(total, cw)

    def forward(k):
        weight_copy(k, 0).wait()
        weight_copy(k, 1).wait()
        tk = token_chunk(k)

        def step(t):
            span = pl.ds(pl.multiple_of(t * tile, 128), tile)
            g = dot(tk, wg[span, k * cw:(k + 1) * cw], 1, 1)
            u = dot(tk, wu[span, k * cw:(k + 1) * cw], 1, 1)
            if k == 0:
                acc_g[:, span] = g
                acc_u[:, span] = u
            else:
                acc_g[:, span] += g
                acc_u[:, span] += u

        each(0, hidden // tile, step)

    own_codes = jnp.zeros((rank, total), F32)
    for i in range(CHUNKS + 2):
        if i < CHUNKS:
            gathers[i].on_z()
        if i == 0:
            map_reduce.on_c()
        if 0 <= i - 1 < CHUNKS:
            gathers[i - 1].on_y()
        if i >= 2:
            k = i - 2
            gathers[k].on_c()
            own_codes = own_codes + dot(
                down_ref[:, k * cw:(k + 1) * cw], token_chunk(k), 1, 1
            )
            if k == CHUNKS - 1:
                code_sum = Sum(codes_buf, code_sem)
                codes_buf[0] = (own_codes * token_chosen).astype(BF16)
                code_sum.start()
                code_sum.on_c()
            forward(k)
            if k == min(1, CHUNKS - 1):
                map_reduce.on_y()

    code_sum.on_y()
    maps[...] = map_reduce.result().astype(BF16)
    codes = code_sum.result()

    for b in range(blocks):
        tokens_b = slice(b * BLOCK, (b + 1) * BLOCK)
        codes_b = codes[:, tokens_b]
        live = lax.broadcasted_iota(jnp.int32, (BLOCK, 1), 0) < live_ref[b]

        def activate(t, b=b, tokens_b=tokens_b, codes_b=codes_b, live=live):
            span = pl.ds(pl.multiple_of(t * half, 128), half)
            map_b = maps[b * rank:(b + 1) * rank, span]
            gate = acc_g[tokens_b, span] + ADAPTER_SCALE * dot(codes_b, map_b, 0, 0)
            s = 1.0 / (1.0 + jnp.exp(-gate))
            grad = jnp.where(live, hid_ref[tokens_b, span].astype(F32), 0.0)
            grad_s = grad * s
            dgate[tokens_b, span] = (
                grad_s * acc_u[tokens_b, span] * (1.0 + gate * (1.0 - s))
            ).astype(BF16)
            dup[tokens_b, span] = (grad_s * gate).astype(BF16)

        each(0, hidden // half, activate)

    cgrad_sum = Sum(cgrad_buf, cgrad_sem)
    for b in range(blocks):
        tokens_b = slice(b * BLOCK, (b + 1) * BLOCK)
        cgrad_buf[0, :, tokens_b] = dot(
            maps[b * rank:(b + 1) * rank, :], dgate[tokens_b, :], 1, 1
        )
    cgrad_sum.start()
    for b in range(blocks):
        tokens_b = slice(b * BLOCK, (b + 1) * BLOCK)
        ugrad_buf[me, b * rank:(b + 1) * rank, :] = (
            ADAPTER_SCALE * dot(codes[:, tokens_b], dgate[tokens_b, :], 1, 0)
        ).astype(BF16)
    ugather = Gather(lambda shard: ugrad_buf.at[shard], uz_sem, uy_sem, uc_sem, 0)
    ugather.start()
    cgrad_sum.on_c()

    ct = 256 if cw % 256 == 0 else 128

    def backward(k):
        def step(t):
            cols = pl.ds(pl.multiple_of(k * cw + t * ct, 128), ct)
            value = dot(dgate[...], wg[:, cols], 1, 0) + dot(dup[...], wu[:, cols], 1, 0)
            part[k, :, :, pl.ds(pl.multiple_of(t * ct, 128), ct)] = value.reshape(n, rows, ct)

        each(0, cw // ct, step)

    def add_adapter(k, cg):
        def step(t):
            cols = pl.ds(pl.multiple_of(k * cw + t * ct, 128), ct)
            span = pl.ds(pl.multiple_of(t * ct, 128), ct)
            value = ADAPTER_SCALE * dot(cg, down_ref[:, cols], 0, 0)
            part[k, :, :, span] += value.reshape(n, rows, ct)

        each(0, cw // ct, step)

    reduces = [
        Reduce(
            lambda i, k=k: part[k, i],
            (cs_buf, cr_buf, ys_buf, yr_buf, zs_buf, zr_buf),
            (rc_sem, ry_sem, rz_sem),
            k,
        )
        for k in range(CHUNKS)
    ]

    def store(k):
        din_ref[:, k * cw:(k + 1) * cw] = reduces[k].result().astype(BF16)

    backward(0)
    cgrad_sum.on_y()
    ugather.on_z()
    if CHUNKS > 1:
        backward(1)
    cg = cgrad_sum.result().astype(F32)
    cg = (cg * token_chosen).astype(BF16)
    for i in range(CHUNKS):
        if i >= 2:
            backward(i)
        add_adapter(i, cg)
        reduces[i].start()
        if i == 1:
            ugather.on_y()
        if i >= 1:
            reduces[i - 1].on_c()
        if i >= 2:
            reduces[i - 2].on_y()
        if i >= 3:
            store(i - 3)
    last = CHUNKS - 1
    reduces[last].on_c()
    if last >= 1:
        reduces[last - 1].on_y()

    for k in range(CHUNKS):
        ddown_ref[:, k * cw:(k + 1) * cw] = (
            ADAPTER_SCALE * dot(cg, token_chunk(k), 1, 0)
        ).astype(BF16)
    reduces[last].on_y()

    ugather.on_c()

    def put(d):
        value = jnp.zeros((rank, hidden), F32)
        for b in range(blocks):
            value = value + chosen[b] * ugrad_buf[d, b * rank:(b + 1) * rank, :].astype(F32)
        dmaps_ref[:, pl.ds(pl.multiple_of(d * hidden, 128), hidden)] = value.astype(BF16)

    each(0, n, put)
    for k in range(max(0, CHUNKS - 3), CHUNKS):
        store(k)
    for g in gathers:
        g.finish()
    ugather.finish()
    map_reduce.finish()
    code_sum.finish()
    cgrad_sum.finish()
    for r in reduces:
        r.finish()


def body(
    nrow,
    ncol,
    tokens,
    hidden_gradient,
    gate_projection_weight,
    up_projection_weight,
    adapter_down_maps,
    adapter_up_maps,
    padded_block_tenant,
    tenant_adapter_slot,
    block_live_count,
):
    n = nrow * ncol
    ny = 2 if ncol == 1 else 1
    nz = n // (2 * ny)
    rows = tokens.shape[0] // ncol
    if ncol > 1:
        tokens = lax.dynamic_slice_in_dim(tokens, lax.axis_index("col") * rows, rows, 0)
    width = tokens.shape[1]
    total = n * rows
    hidden = gate_projection_weight.shape[0]
    rank = adapter_up_maps.shape[1]
    blocks = total // BLOCK
    cw = width // CHUNKS
    mr = blocks * rank
    half = nz * ny
    vmem = pl.BlockSpec(memory_space=pltpu.VMEM)
    smem = pl.BlockSpec(memory_space=pltpu.SMEM)
    hbm = pl.BlockSpec(memory_space=pl.ANY)
    sem = pltpu.SemaphoreType.DMA
    scratch = [
        pltpu.VMEM((hidden, width), BF16),
        pltpu.VMEM((hidden, width), BF16),
        pltpu.VMEM((n, rows, width), BF16),
        pltpu.VMEM((total, hidden), F32),
        pltpu.VMEM((total, hidden), F32),
        pltpu.VMEM((total, hidden), BF16),
        pltpu.VMEM((total, hidden), BF16),
        pltpu.VMEM((CHUNKS, n, rows, cw), F32),
        pltpu.VMEM((CHUNKS, half, rows, cw), BF16),
        pltpu.VMEM((CHUNKS, half, rows, cw), BF16),
        pltpu.VMEM((CHUNKS, nz, rows, cw), BF16),
        pltpu.VMEM((CHUNKS, nz, rows, cw), BF16),
        pltpu.VMEM((CHUNKS, nz, rows, cw), BF16),
        pltpu.VMEM((CHUNKS, nz, rows, cw), BF16),
        pltpu.VMEM((1, half, mr, hidden), BF16),
        pltpu.VMEM((1, half, mr, hidden), BF16),
        pltpu.VMEM((1, nz, mr, hidden), BF16),
        pltpu.VMEM((1, nz, mr, hidden), BF16),
        pltpu.VMEM((1, nz, mr, hidden), BF16),
        pltpu.VMEM((1, nz, mr, hidden), BF16),
        pltpu.VMEM((mr, hidden), BF16),
        pltpu.VMEM((4 + nz, rank, total), BF16),
        pltpu.VMEM((4 + nz, rank, total), F32),
        pltpu.VMEM((n, mr, hidden), BF16),
        sem((CHUNKS, 2)),
        sem((2, CHUNKS, nz)),
        sem((2, CHUNKS, nz)),
        sem((2, CHUNKS, half)),
        sem((2, 1, nz)),
        sem((2, 1, nz)),
        sem((2, 1, half)),
        sem((2, CHUNKS)),
        sem((2, CHUNKS)),
        sem((2, CHUNKS, nz)),
        sem((2, 1)),
        sem((2, 1)),
        sem((2, 1, nz)),
        sem((2, 1 + nz)),
        sem((2, 1 + nz)),
    ]
    input_gradient, down_t, up_grad = pl.pallas_call(
        functools.partial(kernel, (nz, ny, ncol)),
        out_shape=(
            jax.ShapeDtypeStruct((rows, width), BF16),
            jax.ShapeDtypeStruct((rank, width), BF16),
            jax.ShapeDtypeStruct((rank, n * hidden), BF16),
        ),
        in_specs=[vmem, vmem, hbm, hbm, vmem, vmem, smem, smem, smem],
        out_specs=(vmem, vmem, vmem),
        scratch_shapes=scratch,
        compiler_params=pltpu.CompilerParams(
            collective_id=0, has_side_effects=True, vmem_limit_bytes=62 * 1024 * 1024
        ),
    )(
        tokens,
        hidden_gradient,
        gate_projection_weight,
        up_projection_weight,
        jnp.swapaxes(adapter_down_maps[0], 0, 1),
        adapter_up_maps[0],
        padded_block_tenant,
        tenant_adapter_slot,
        block_live_count,
    )
    return input_gradient, jnp.swapaxes(down_t, 0, 1)[None], up_grad[None]


def solution(mesh):
    return jax.shard_map(
        functools.partial(body, mesh.shape["row"], mesh.shape["col"]),
        mesh=mesh,
        in_specs=(
            P(("groups", "row"), None),
            P("groups", ("row", "col")),
            P(("row", "col"), None),
            P(("row", "col"), None),
            P(("groups", "row", "col"), None, None),
            P(("groups", "row", "col"), None, None),
            P("groups"),
            P("groups"),
            P("groups"),
        ),
        out_specs=(
            P(("groups", "row", "col"), None),
            P(("groups", "row", "col"), None, None),
            P(("groups", "row", "col"), None, None),
        ),
        check_vma=False,
    )
```

```python
import functools

import jax
import jax.numpy as jnp
from jax import lax
from jax.experimental import pallas as pl
from jax.experimental.pallas import tpu as pltpu
from jax.sharding import PartitionSpec as P

BLOCK = 128
ADAPTER_SCALE = 0.5
CHUNKS = 4
BF16 = jnp.bfloat16
F32 = jnp.float32


def dot(a, b, ca, cb):
    return lax.dot_general(a, b, (((ca,), (cb,)), ((), ())), preferred_element_type=F32)


def each(lo, hi, body):
    def step(i, carry):
        body(i)
        return carry

    lax.fori_loop(lo, hi, step, 0)


def kernel(
    dims,
    tok_in, hid_ref, gate_hbm, up_hbm, down_ref, maps_ref, tenant_ref, slot_ref, live_ref,
    din_ref, ddown_ref, dmaps_ref,
    wg, wu, tok, acc_g, acc_u, dgate, dup, part,
    cs_buf, cr_buf, ys_buf, yr_buf, zs_buf, zr_buf,
    mcs_buf, mcr_buf, mys_buf, myr_buf, mzs_buf, mzr_buf, maps,
    codes_buf, cgrad_buf, ugrad_buf,
    w_sem, tz_sem, ty_sem, tc_sem, uz_sem, uy_sem, uc_sem,
    rc_sem, ry_sem, rz_sem, mc_sem, my_sem, mz_sem, code_sem, cgrad_sem,
):
    nz, ny, ncol = dims
    n = nz * ny * 2
    rows, width = tok_in.shape
    total = n * rows
    blocks = total // BLOCK
    hidden = wg.shape[0]
    rank = down_ref.shape[0]
    cw = width // CHUNKS
    me = lax.axis_index("row") * ncol + lax.axis_index("col")
    z, y, c = me // (2 * ny), (me // 2) % ny, me % 2

    def index(zz, yy, cc):
        return (zz * ny + yy) * 2 + cc

    def device(i):
        return {"row": i // ncol, "col": i % ncol}

    def remote(src, dst, sems, target):
        return pltpu.make_async_remote_copy(
            src_ref=src,
            dst_ref=dst,
            send_sem=sems[0],
            recv_sem=sems[1],
            device_id=device(target),
            device_id_type=pl.DeviceIdType.MESH,
        )

    y_peer, c_peer = index(z, ny - 1 - y, c), index(z, y, 1 - c)

    def weight_copy(k, which):
        src, dst = ((gate_hbm, wg), (up_hbm, wu))[which]
        cols = pl.ds(k * cw, cw)
        return pltpu.make_async_copy(src.at[:, cols], dst.at[:, cols], w_sem.at[k, which])

    for k in range(CHUNKS):
        for which in range(2):
            weight_copy(k, which).start()

    barrier = pltpu.get_barrier_semaphore()

    def greet(d):
        pl.semaphore_signal(
            barrier, inc=1, device_id=device((me + d) % n), device_id_type=pl.DeviceIdType.MESH
        )

    each(1, n, greet)
    tok[me] = tok_in[...]
    pl.semaphore_wait(barrier, n - 1)

    class Gather:
        def __init__(self, view, zsem, ysem, csem, k):
            self.view, self.k = view, k
            self.zsem, self.ysem, self.csem = zsem, ysem, csem

        def z_copy(self, d, shard):
            sems = (self.zsem.at[0, self.k, d], self.zsem.at[1, self.k, d])
            v = self.view(shard)
            return remote(v, v, sems, index((z + d) % nz, y, c))

        def y_copy(self, d, shard):
            sems = (self.ysem.at[0, self.k, d], self.ysem.at[1, self.k, d])
            v = self.view(shard)
            return remote(v, v, sems, y_peer)

        def c_copy(self, j, shard):
            sems = (self.csem.at[0, self.k, j], self.csem.at[1, self.k, j])
            v = self.view(shard)
            return remote(v, v, sems, c_peer)

        def start(self):
            each(1, nz, lambda d: self.z_copy(d, me).start())
            if ny > 1:
                self.y_copy(0, me).start()
            self.c_copy(0, me).start()

        def on_z(self):
            def arrived(d):
                shard = index((z + nz - d) % nz, y, c)
                self.z_copy(d, shard).wait_recv()
                if ny > 1:
                    self.y_copy(d, shard).start()
                self.c_copy(d, shard).start()

            each(1, nz, arrived)

        def on_y(self):
            def arrived(d):
                shard = index((z + nz - d) % nz, ny - 1 - y, c)
                self.y_copy(d, shard).wait_recv()
                self.c_copy(nz + d, shard).start()

            if ny > 1:
                each(0, nz, arrived)

        def on_c(self):
            each(0, nz * ny, lambda j: self.c_copy(j, me).wait_recv())

        def finish(self):
            each(1, nz, lambda d: self.z_copy(d, me).wait_send())
            if ny > 1:
                each(0, nz, lambda d: self.y_copy(d, me).wait_send())
            each(0, nz * ny, lambda j: self.c_copy(j, me).wait_send())

    class Reduce:
        def __init__(self, piece, bufs, sems, k):
            self.piece, self.k = piece, k
            self.cs, self.cr, self.ys, self.yr, self.zs, self.zr = [b.at[k] for b in bufs]
            csem, ysem, zsem = sems
            self.c_copy = remote(self.cs, self.cr, (csem.at[0, k], csem.at[1, k]), c_peer)
            self.y_copy = remote(self.ys, self.yr, (ysem.at[0, k], ysem.at[1, k]), y_peer)
            self.zsem = zsem

        def z_copy(self, d):
            sems = (self.zsem.at[0, self.k, d], self.zsem.at[1, self.k, d])
            return remote(self.zs.at[d], self.zr.at[d], sems, index((z + d) % nz, y, c))

        def start(self):
            def fill(j):
                self.cs[j] = self.piece(j * 2 + 1 - c).astype(BF16)

            each(0, nz * ny, fill)
            self.c_copy.start()

        def chip_sum(self, zz, yy):
            return self.piece(index(zz, yy, c)) + self.cr[zz * ny + yy].astype(F32)

        def on_c(self):
            self.c_copy.wait_recv()

            def fill(zz):
                self.ys[zz] = self.chip_sum(zz, ny - 1 - y).astype(BF16)

            if ny > 1:
                each(0, nz, fill)
                self.y_copy.start()

        def y_sum(self, zz):
            value = self.chip_sum(zz, y)
            if ny > 1:
                value = value + self.yr[zz].astype(F32)
            return value

        def on_y(self):
            if ny > 1:
                self.y_copy.wait_recv()

            def send(d):
                self.zs[d] = self.y_sum((z + d) % nz).astype(BF16)
                self.z_copy(d).start()

            each(1, nz, send)

        def result(self):
            def add(d, value):
                self.z_copy(d).wait_recv()
                return value + self.zr[d].astype(F32)

            return lax.fori_loop(1, nz, add, self.y_sum(z))

        def finish(self):
            self.c_copy.wait_send()
            if ny > 1:
                self.y_copy.wait_send()
            each(1, nz, lambda d: self.z_copy(d).wait_send())

    class Sum:
        def __init__(self, buf, sem):
            self.buf, self.sem = buf, sem

        def pair(self, i, target):
            sems = (self.sem.at[0, i], self.sem.at[1, i])
            return remote(self.buf.at[2 * i], self.buf.at[2 * i + 1], sems, target)

        def z_copy(self, d):
            sems = (self.sem.at[0, 1 + d], self.sem.at[1, 1 + d])
            return remote(self.buf.at[4], self.buf.at[4 + d], sems, index((z + d) % nz, y, c))

        def start(self):
            self.pair(0, c_peer).start()

        def on_c(self):
            self.pair(0, c_peer).wait_recv()
            value = self.buf[0].astype(F32) + self.buf[1].astype(F32)
            self.buf[2] = value.astype(self.buf.dtype)
            if ny > 1:
                self.pair(1, y_peer).start()

        def on_y(self):
            value = self.buf[2].astype(F32)
            if ny > 1:
                self.pair(1, y_peer).wait_recv()
                value = value + self.buf[3].astype(F32)
            self.buf[4] = value.astype(self.buf.dtype)
            each(1, nz, lambda d: self.z_copy(d).start())

        def result(self):
            each(1, nz, lambda d: self.z_copy(d).wait_recv())
            return jnp.sum(self.buf[4:4 + nz].astype(F32), axis=0).astype(BF16)

        def finish(self):
            self.pair(0, c_peer).wait_send()
            if ny > 1:
                self.pair(1, y_peer).wait_send()
            each(1, nz, lambda d: self.z_copy(d).wait_send())

    slots = [slot_ref[tenant_ref[b]] for b in range(blocks)]
    chosen = [jnp.where(s == me, 1.0, 0.0).astype(F32) for s in slots]
    token_block = lax.broadcasted_iota(jnp.int32, (1, total), 1) // BLOCK
    token_chosen = jnp.zeros((1, total), F32)
    for b in range(blocks):
        token_chosen = jnp.where(token_block == b, chosen[b], token_chosen)

    def map_piece(i):
        cols = pl.ds(pl.multiple_of(i * hidden, 128), hidden)
        one = maps_ref[:, cols].astype(F32)
        return jnp.concatenate([one * chosen[b] for b in range(blocks)], axis=0)

    map_reduce = Reduce(
        map_piece,
        (mcs_buf, mcr_buf, mys_buf, myr_buf, mzs_buf, mzr_buf),
        (mc_sem, my_sem, mz_sem),
        0,
    )
    gathers = [
        Gather(
            lambda shard, k=k: tok.at[shard, :, pl.ds(k * cw, cw)], tz_sem, ty_sem, tc_sem, k
        )
        for k in range(CHUNKS)
    ]

    for g in gathers:
        g.start()
    map_reduce.start()

    tile = min(hidden, 512)
    half = min(hidden, 256) if hidden % 256 == 0 else 128

    def token_chunk(k):
        return tok[:, :, k * cw:(k + 1) * cw].reshape(total, cw)

    def forward(k, between=()):
        weight_copy(k, 0).wait()
        weight_copy(k, 1).wait()
        tk = token_chunk(k)

        def step(t):
            span = pl.ds(pl.multiple_of(t * tile, 128), tile)
            g = dot(tk, wg[span, k * cw:(k + 1) * cw], 1, 1)
            u = dot(tk, wu[span, k * cw:(k + 1) * cw], 1, 1)
            if k == 0:
                acc_g[:, span] = g
                acc_u[:, span] = u
            else:
                acc_g[:, span] += g
                acc_u[:, span] += u

        tiles = hidden // tile
        at = 0
        for action in between:
            if at < tiles:
                each(at, at + 1, step)
                at += 1
            action()
        each(at, tiles, step)

    own_codes = jnp.zeros((rank, total), F32)
    for i in range(CHUNKS + 2):
        if i < CHUNKS:
            gathers[i].on_z()
        if i == 0:
            map_reduce.on_c()
        if 0 <= i - 1 < CHUNKS:
            gathers[i - 1].on_y()
        if i >= 2:
            k = i - 2
            gathers[k].on_c()
            own_codes = own_codes + dot(
                down_ref[:, k * cw:(k + 1) * cw], token_chunk(k), 1, 1
            )
            if k == CHUNKS - 1:
                code_sum = Sum(codes_buf, code_sem)
                codes_buf[0] = (own_codes * token_chosen).astype(BF16)
                code_sum.start()
                forward(k, (code_sum.on_c, code_sum.on_y))
            else:
                forward(k)
            if k == min(1, CHUNKS - 1):
                map_reduce.on_y()

    maps[...] = map_reduce.result().astype(BF16)
    codes = code_sum.result()

    for b in range(blocks):
        tokens_b = slice(b * BLOCK, (b + 1) * BLOCK)
        codes_b = codes[:, tokens_b]
        live = lax.broadcasted_iota(jnp.int32, (BLOCK, 1), 0) < live_ref[b]

        def activate(t, b=b, tokens_b=tokens_b, codes_b=codes_b, live=live):
            span = pl.ds(pl.multiple_of(t * half, 128), half)
            map_b = maps[b * rank:(b + 1) * rank, span]
            gate = acc_g[tokens_b, span] + ADAPTER_SCALE * dot(codes_b, map_b, 0, 0)
            s = 1.0 / (1.0 + jnp.exp(-gate))
            grad = jnp.where(live, hid_ref[tokens_b, span].astype(F32), 0.0)
            grad_s = grad * s
            dgate[tokens_b, span] = (
                grad_s * acc_u[tokens_b, span] * (1.0 + gate * (1.0 - s))
            ).astype(BF16)
            dup[tokens_b, span] = (grad_s * gate).astype(BF16)

        each(0, hidden // half, activate)

    cgrad_sum = Sum(cgrad_buf, cgrad_sem)
    for b in range(blocks):
        tokens_b = slice(b * BLOCK, (b + 1) * BLOCK)
        cgrad_buf[0, :, tokens_b] = dot(
            maps[b * rank:(b + 1) * rank, :], dgate[tokens_b, :], 1, 1
        )
    cgrad_sum.start()
    for b in range(blocks):
        tokens_b = slice(b * BLOCK, (b + 1) * BLOCK)
        ugrad_buf[me, b * rank:(b + 1) * rank, :] = (
            ADAPTER_SCALE * dot(codes[:, tokens_b], dgate[tokens_b, :], 1, 0)
        ).astype(BF16)
    ugather = Gather(lambda shard: ugrad_buf.at[shard], uz_sem, uy_sem, uc_sem, 0)
    ugather.start()
    cgrad_sum.on_c()

    ct = 256 if cw % 256 == 0 else 128

    def backward(k):
        def step(t):
            cols = pl.ds(pl.multiple_of(k * cw + t * ct, 128), ct)
            value = dot(dgate[...], wg[:, cols], 1, 0) + dot(dup[...], wu[:, cols], 1, 0)
            part[k, :, :, pl.ds(pl.multiple_of(t * ct, 128), ct)] = value.reshape(n, rows, ct)

        each(0, cw // ct, step)

    def add_adapter(k, cg):
        def step(t):
            cols = pl.ds(pl.multiple_of(k * cw + t * ct, 128), ct)
            span = pl.ds(pl.multiple_of(t * ct, 128), ct)
            value = ADAPTER_SCALE * dot(cg, down_ref[:, cols], 0, 0)
            part[k, :, :, span] += value.reshape(n, rows, ct)

        each(0, cw // ct, step)

    reduces = [
        Reduce(
            lambda i, k=k: part[k, i],
            (cs_buf, cr_buf, ys_buf, yr_buf, zs_buf, zr_buf),
            (rc_sem, ry_sem, rz_sem),
            k,
        )
        for k in range(CHUNKS)
    ]

    def store(k):
        din_ref[:, k * cw:(k + 1) * cw] = reduces[k].result().astype(BF16)

    backward(0)
    cgrad_sum.on_y()
    ugather.on_z()
    if CHUNKS > 1:
        backward(1)
    cg = cgrad_sum.result().astype(F32)
    cg = (cg * token_chosen).astype(BF16)
    for i in range(CHUNKS):
        if i >= 2:
            backward(i)
        add_adapter(i, cg)
        reduces[i].start()
        if i == 1:
            ugather.on_y()
        if i >= 1:
            reduces[i - 1].on_c()
        if i >= 2:
            reduces[i - 2].on_y()
        if i >= 3:
            store(i - 3)
    last = CHUNKS - 1
    reduces[last].on_c()
    if last >= 1:
        reduces[last - 1].on_y()

    for k in range(CHUNKS):
        ddown_ref[:, k * cw:(k + 1) * cw] = (
            ADAPTER_SCALE * dot(cg, token_chunk(k), 1, 0)
        ).astype(BF16)
    reduces[last].on_y()

    ugather.on_c()

    def put(d):
        value = jnp.zeros((rank, hidden), F32)
        for b in range(blocks):
            value = value + chosen[b] * ugrad_buf[d, b * rank:(b + 1) * rank, :].astype(F32)
        dmaps_ref[:, pl.ds(pl.multiple_of(d * hidden, 128), hidden)] = value.astype(BF16)

    each(0, n, put)
    for k in range(max(0, CHUNKS - 3), CHUNKS):
        store(k)
    for g in gathers:
        g.finish()
    ugather.finish()
    map_reduce.finish()
    code_sum.finish()
    cgrad_sum.finish()
    for r in reduces:
        r.finish()


def body(
    nrow,
    ncol,
    tokens,
    hidden_gradient,
    gate_projection_weight,
    up_projection_weight,
    adapter_down_maps,
    adapter_up_maps,
    padded_block_tenant,
    tenant_adapter_slot,
    block_live_count,
):
    n = nrow * ncol
    ny = 2 if ncol == 1 else 1
    nz = n // (2 * ny)
    rows = tokens.shape[0] // ncol
    if ncol > 1:
        tokens = lax.dynamic_slice_in_dim(tokens, lax.axis_index("col") * rows, rows, 0)
    width = tokens.shape[1]
    total = n * rows
    hidden = gate_projection_weight.shape[0]
    rank = adapter_up_maps.shape[1]
    blocks = total // BLOCK
    cw = width // CHUNKS
    mr = blocks * rank
    half = nz * ny
    vmem = pl.BlockSpec(memory_space=pltpu.VMEM)
    smem = pl.BlockSpec(memory_space=pltpu.SMEM)
    hbm = pl.BlockSpec(memory_space=pl.ANY)
    sem = pltpu.SemaphoreType.DMA
    scratch = [
        pltpu.VMEM((hidden, width), BF16),
        pltpu.VMEM((hidden, width), BF16),
        pltpu.VMEM((n, rows, width), BF16),
        pltpu.VMEM((total, hidden), F32),
        pltpu.VMEM((total, hidden), F32),
        pltpu.VMEM((total, hidden), BF16),
        pltpu.VMEM((total, hidden), BF16),
        pltpu.VMEM((CHUNKS, n, rows, cw), F32),
        pltpu.VMEM((CHUNKS, half, rows, cw), BF16),
        pltpu.VMEM((CHUNKS, half, rows, cw), BF16),
        pltpu.VMEM((CHUNKS, nz, rows, cw), BF16),
        pltpu.VMEM((CHUNKS, nz, rows, cw), BF16),
        pltpu.VMEM((CHUNKS, nz, rows, cw), BF16),
        pltpu.VMEM((CHUNKS, nz, rows, cw), BF16),
        pltpu.VMEM((1, half, mr, hidden), BF16),
        pltpu.VMEM((1, half, mr, hidden), BF16),
        pltpu.VMEM((1, nz, mr, hidden), BF16),
        pltpu.VMEM((1, nz, mr, hidden), BF16),
        pltpu.VMEM((1, nz, mr, hidden), BF16),
        pltpu.VMEM((1, nz, mr, hidden), BF16),
        pltpu.VMEM((mr, hidden), BF16),
        pltpu.VMEM((4 + nz, rank, total), BF16),
        pltpu.VMEM((4 + nz, rank, total), F32),
        pltpu.VMEM((n, mr, hidden), BF16),
        sem((CHUNKS, 2)),
        sem((2, CHUNKS, nz)),
        sem((2, CHUNKS, nz)),
        sem((2, CHUNKS, half)),
        sem((2, 1, nz)),
        sem((2, 1, nz)),
        sem((2, 1, half)),
        sem((2, CHUNKS)),
        sem((2, CHUNKS)),
        sem((2, CHUNKS, nz)),
        sem((2, 1)),
        sem((2, 1)),
        sem((2, 1, nz)),
        sem((2, 1 + nz)),
        sem((2, 1 + nz)),
    ]
    input_gradient, down_t, up_grad = pl.pallas_call(
        functools.partial(kernel, (nz, ny, ncol)),
        out_shape=(
            jax.ShapeDtypeStruct((rows, width), BF16),
            jax.ShapeDtypeStruct((rank, width), BF16),
            jax.ShapeDtypeStruct((rank, n * hidden), BF16),
        ),
        in_specs=[vmem, vmem, hbm, hbm, vmem, vmem, smem, smem, smem],
        out_specs=(vmem, vmem, vmem),
        scratch_shapes=scratch,
        compiler_params=pltpu.CompilerParams(
            collective_id=0, has_side_effects=True, vmem_limit_bytes=62 * 1024 * 1024
        ),
    )(
        tokens,
        hidden_gradient,
        gate_projection_weight,
        up_projection_weight,
        jnp.swapaxes(adapter_down_maps[0], 0, 1),
        adapter_up_maps[0],
        padded_block_tenant,
        tenant_adapter_slot,
        block_live_count,
    )
    return input_gradient, jnp.swapaxes(down_t, 0, 1)[None], up_grad[None]


def solution(mesh):
    return jax.shard_map(
        functools.partial(body, mesh.shape["row"], mesh.shape["col"]),
        mesh=mesh,
        in_specs=(
            P(("groups", "row"), None),
            P("groups", ("row", "col")),
            P(("row", "col"), None),
            P(("row", "col"), None),
            P(("groups", "row", "col"), None, None),
            P(("groups", "row", "col"), None, None),
            P("groups"),
            P("groups"),
            P("groups"),
        ),
        out_specs=(
            P(("groups", "row", "col"), None),
            P(("groups", "row", "col"), None, None),
            P(("groups", "row", "col"), None, None),
        ),
        check_vma=False,
    )
```
